32 devices in a mesh: members: 2 (over x), band: 16 (over z, y, core).
Axes of the slice: x: 2, y: 2, z: 4, core: 2. Of those that a mesh axis runs over, the one named last changes fastest.
Arguments:
- grid_inputs: bfloat16 [96, 384, 256], P(('members', 'band')), parts along dimension 0, may hold values from -6 to 6
- stencil_prenorm_scale: float32 [256], replicated, may hold values from 0.1 to 1.9
- patch_kernel_profiles: float32 [48, 9, 27], P('band'), may hold values from -1.2 to 1.2
- channel_mixer_tensor: bfloat16 [2304, 256], replicated, may hold values from -0.125 to 0.125
- softmax_prenorm_scale: float32 [256], replicated, may hold values from 0.1 to 1.9
- probe_lookup_content_projector: bfloat16 [256, 768], replicated, may hold values from -0.375 to 0.375
- head_logit_scales: float32 [8], replicated, may hold values from 3 to 500
- final_projector: bfloat16 [256, 256], replicated, may hold values from -0.375 to 0.375
- azimuth_reaches: int32 [48, 5], P('band'), may hold values from 1 to 8, as said below
Outputs:
- encoded: bfloat16 [96, 384, 256], P(('members', 'band')), parts along dimension 0
The draws below stay inside these ranges and needn't reach their ends.
There are 2 independent parts, one for each index of `members`. The reference program is written for one: setup_inputs(seed, part) draws one part's arguments, and reference() takes and returns one part's arrays. A program takes and returns all parts, laid end to end along the dimension named above; an argument that names none is the same for every part. Nothing has to cross between parts.
Inputs may be any that keep to these rules, and one draw needn't show every extreme that they name: azimuth_reaches[i, a] is the longitude reach of row i's disc in its row at offset a - 2; the rows at the poles reach 8.
All inputs are finite; a program needn't handle non-finite values.
Results may differ from the reference program's by a relative error of at most 0.025.
The reference program's roundings to bfloat16 on the way count: a program that leaves them out, or rounds other values in their place, can miss the bound.
Values may be sent and summed in bfloat16 or wider, within the bound.
A program may use at most 64 MiB of HBM per device.

```python
import math
import jax
import jax.numpy as jnp
from jax import lax

LONGITUDES = 384
HEAD_COUNT = 8
HEAD_WIDTH = 32
CHANNELS = 256
BASIS_COUNT = 9
CONV_REACH = 4
PATCH_LAT_EXTENT = 2
DISC_REACH = 8
QUERY_BLOCK = 48
LATITUDES = 48


def draw_head_logit_scales(key, part):
    first = jax.random.fold_in(key, 0)
    gentle = jnp.exp(jax.random.uniform(first, (HEAD_COUNT,), jnp.float32, math.log(3.0), math.log(12.0)))
    return gentle


def draw_azimuth_reaches(key, part):
    row_ids = jnp.arange(LATITUDES, dtype=jnp.int32)
    distance = jnp.abs(2 * row_ids - (LATITUDES - 1))
    edge_row = LATITUDES - 1
    base_span = 1 + DISC_REACH * distance * distance // (edge_row * edge_row)
    jitter = jax.random.randint(key, (LATITUDES, 2 * PATCH_LAT_EXTENT + 1), 0, 2, dtype=jnp.int32)
    return jnp.minimum(DISC_REACH, base_span[:, None] + jitter).astype(jnp.int32)


def steps_of(key, dims, cuts, least, top_value):
    factor_of = 1.0
    for axis_at, shards_of in cuts:
        steps = jax.random.uniform(jax.random.fold_in(jax.random.fold_in(key, 6), axis_at), (shards_of,), jnp.float32, least / len(cuts), top_value / len(cuts))
        factor_of = factor_of * jnp.repeat(jnp.exp(steps), dims[axis_at] // shards_of).reshape((-1,) + (1,) * (len(dims) - 1 - axis_at))
    return factor_of


def normal_values(stream_key, dims, scale, limit, cuts=(), held_as=jnp.bfloat16):
    factor_of = steps_of(stream_key, dims, cuts, -0.22, 0.18) if cuts else 1.0
    array = jax.random.normal(stream_key, dims, jnp.float32) * scale * factor_of
    return jnp.minimum(jnp.maximum(array, -limit), limit).astype(held_as)


def setup_inputs(seed: int = 0, part: int = 0) -> dict:
    splits = jax.random.split(jax.random.key(seed), 10)
    own_keys = jax.random.split(jax.random.fold_in(splits[9], part), 10)
    return {
        "grid_inputs": normal_values(own_keys[0], (LATITUDES, LONGITUDES, CHANNELS), 1.0, 6.0, ((0, 16),)),
        "stencil_prenorm_scale": jnp.clip(1.0 + 0.18 * jax.random.normal(splits[1], (CHANNELS,), jnp.float32), 0.1, 1.9),
        "patch_kernel_profiles": normal_values(splits[2], (LATITUDES, BASIS_COUNT, 3 * (2 * CONV_REACH + 1)), 0.2, 1.2, ((0, 16),), jnp.float32),
        "channel_mixer_tensor": normal_values(splits[3], (BASIS_COUNT * CHANNELS, CHANNELS), (BASIS_COUNT * CHANNELS) ** -0.5, 0.125),
        "softmax_prenorm_scale": jnp.clip(1.0 + 0.18 * jax.random.normal(splits[4], (CHANNELS,), jnp.float32), 0.1, 1.9),
        "probe_lookup_content_projector": normal_values(splits[5], (CHANNELS, 3 * CHANNELS), CHANNELS ** -0.5, 0.375),
        "head_logit_scales": draw_head_logit_scales(jax.random.fold_in(splits[9], 71), part),
        "final_projector": normal_values(splits[7], (CHANNELS, CHANNELS), CHANNELS ** -0.5, 0.375),
        "azimuth_reaches": draw_azimuth_reaches(jax.random.fold_in(splits[9], 71), part),
    }


EPSILON = 1e-06

def rms_norm(values, gain_vector):
    values = values.astype(jnp.float32)
    inverse = lax.rsqrt(lax.optimization_barrier(jnp.mean(values * values, axis=-1, keepdims=True)) + EPSILON)
    return values * inverse * gain_vector

def reflect(rim_rows):
    return jnp.roll(jnp.flip(rim_rows, axis=-3), rim_rows.shape[-2] // 2, axis=-2)

def pole_extend(field_rows, rim_width):
    return jnp.concatenate([reflect(field_rows[:rim_width]), field_rows, reflect(field_rows[-rim_width:])], axis=0)

def unit_heads(values):
    shaped = values.astype(jnp.float32).reshape(values.shape[:-1] + (HEAD_COUNT, HEAD_WIDTH))
    inverse = lax.rsqrt(lax.optimization_barrier(jnp.sum(shaped * shaped, axis=-1, keepdims=True)) + EPSILON)
    return (shaped * inverse).reshape(values.shape).astype(jnp.bfloat16)

def conv_filters(patch_kernel_profiles, azimuth_reaches):
    tap_count = 2 * CONV_REACH + 1
    offsets = jnp.abs(jnp.arange(tap_count, dtype=jnp.int32) - CONV_REACH)
    limits = azimuth_reaches[:, PATCH_LAT_EXTENT - 1:PATCH_LAT_EXTENT + 2]
    visible = offsets[None, None, :] <= limits[:, :, None]
    shaped = patch_kernel_profiles.reshape(patch_kernel_profiles.shape[0], BASIS_COUNT, 3, tap_count)
    masked = jnp.where(visible[:, None], shaped, jnp.float32(0.0))
    return masked.astype(jnp.bfloat16).reshape(patch_kernel_profiles.shape)

def lon_taps(window):
    shifted = jnp.stack([jnp.roll(window, CONV_REACH - offset, axis=1) for offset in range(2 * CONV_REACH + 1)], axis=1)
    return shifted.reshape((-1,) + window.shape[1:])

def lon_windows(rim_rows):
    padded = jnp.concatenate([rim_rows[:, -DISC_REACH:], rim_rows, rim_rows[:, :QUERY_BLOCK - DISC_REACH]], axis=1)
    blocks = padded.reshape(padded.shape[0], -1, QUERY_BLOCK, padded.shape[-1])
    windows = jnp.concatenate([blocks[:, :-1], blocks[:, 1:, :2 * DISC_REACH]], axis=2)
    return windows.reshape(windows.shape[:3] + (HEAD_COUNT, HEAD_WIDTH))

def look_at_one_parallel(lone_probe_parallel, lookup_strip_parallels, content_strip_parallels, parallel_azimuth_reach, head_logit_scales):
    window_width = QUERY_BLOCK + 2 * DISC_REACH
    probe_tensor = lone_probe_parallel.astype(jnp.float32).reshape(-1, QUERY_BLOCK, HEAD_COUNT, HEAD_WIDTH)
    lookup_patch_neighbours = lon_windows(lookup_strip_parallels).astype(jnp.float32)
    value_windows = lon_windows(content_strip_parallels).astype(jnp.float32)
    similarity_logits = jnp.einsum('kyge,wknge->kgywn', probe_tensor, lookup_patch_neighbours) * head_logit_scales[None, :, None, None, None]
    positions = jnp.arange(QUERY_BLOCK, dtype=jnp.int32)
    columns = jnp.arange(window_width, dtype=jnp.int32)
    distance = jnp.abs(columns[None, :] - DISC_REACH - positions[:, None])
    visible = distance[:, None, :] <= parallel_azimuth_reach[None, :, None]
    similarity_logits = jnp.where(visible[None, None], similarity_logits, jnp.float32(-1e+30))
    flattened = similarity_logits.reshape(similarity_logits.shape[:3] + (-1,))
    row_peak = lax.optimization_barrier(jnp.max(flattened, axis=-1, keepdims=True))
    exponent = jnp.exp(flattened - row_peak)
    weights = (exponent / lax.optimization_barrier(jnp.sum(exponent, axis=-1, keepdims=True))).astype(jnp.bfloat16).reshape(similarity_logits.shape)
    mixture = jnp.einsum('nhqaw,anwhd->nqhd', weights.astype(jnp.float32), value_windows)
    return mixture.astype(jnp.bfloat16).reshape(LONGITUDES, CHANNELS)

def reference(grid_inputs, stencil_prenorm_scale, patch_kernel_profiles, channel_mixer_tensor, softmax_prenorm_scale, probe_lookup_content_projector, head_logit_scales, final_projector, azimuth_reaches):
    normed = rms_norm(grid_inputs, stencil_prenorm_scale).astype(jnp.bfloat16)
    extended = pole_extend(normed, 1)
    filters = conv_filters(patch_kernel_profiles, azimuth_reaches)

    def conv_row(present_parallel_number):
        window = lax.dynamic_slice_in_dim(extended, present_parallel_number, 3, 0)
        tap_stack = lon_taps(window).astype(jnp.float32)
        basis_sums = jnp.einsum('kt,tjc->jkc', filters[present_parallel_number].astype(jnp.float32), tap_stack).astype(jnp.bfloat16)
        return jnp.dot(basis_sums.reshape(LONGITUDES, -1), channel_mixer_tensor, preferred_element_type=jnp.float32)
    row_ids = jnp.arange(LATITUDES, dtype=jnp.int32)
    hidden = grid_inputs.astype(jnp.float32) + lax.map(conv_row, row_ids)
    attn_in = rms_norm(hidden, softmax_prenorm_scale).astype(jnp.bfloat16)
    projected = jnp.dot(attn_in.reshape(-1, CHANNELS), probe_lookup_content_projector, preferred_element_type=jnp.float32).astype(jnp.bfloat16)
    projected = projected.reshape(LATITUDES, LONGITUDES, 3 * CHANNELS)
    rescaled_probe = unit_heads(projected[..., :CHANNELS])
    lookup_vectors_padded = pole_extend(unit_heads(projected[..., CHANNELS:2 * CHANNELS]), PATCH_LAT_EXTENT)
    content_vectors_padded = pole_extend(projected[..., 2 * CHANNELS:], PATCH_LAT_EXTENT)

    def attend_global(present_parallel_number):
        return look_at_one_parallel(rescaled_probe[present_parallel_number], lax.dynamic_slice_in_dim(lookup_vectors_padded, present_parallel_number, 2 * PATCH_LAT_EXTENT + 1, 0), lax.dynamic_slice_in_dim(content_vectors_padded, present_parallel_number, 2 * PATCH_LAT_EXTENT + 1, 0), azimuth_reaches[present_parallel_number], head_logit_scales)
    mixture = lax.map(attend_global, row_ids)
    output = jnp.dot(mixture.reshape(-1, CHANNELS), final_projector, preferred_element_type=jnp.float32)
    return (hidden + output.reshape(hidden.shape)).astype(jnp.bfloat16)
```

```python
import functools
import math

import jax
import jax.numpy as jnp
from jax import lax
from jax.experimental import pallas as pl
from jax.experimental.pallas import tpu as pltpu
from jax.sharding import PartitionSpec as P

HEAD_COUNT = 8
HEAD_WIDTH = 32
BASIS_COUNT = 9
CONV_REACH = 4
PATCH_LAT_EXTENT = 2
DISC_REACH = 8
EPSILON = 1e-06

TAPS = 2 * CONV_REACH + 1
CONV_BLOCK = 64
CONV_WINDOW = CONV_BLOCK + 16
QUERY_BLOCK = 32
KEY_WINDOW = QUERY_BLOCK + 2 * DISC_REACH
KEYS = 256
ROWS_A = 2 * PATCH_LAT_EXTENT + 1
PAD = DISC_REACH
TAIL = 24
LOG2E = math.log2(math.e)
F32 = jnp.float32
BF16 = jnp.bfloat16


def rms(values, gain):
    inverse = lax.rsqrt(jnp.mean(values * values, axis=-1, keepdims=True) + EPSILON)
    return values * inverse * gain


def ring_pad(row):
    return jnp.concatenate([row[-PAD:], row, row[:TAIL]], axis=0)


def half_turn(row):
    half = row.shape[0] // 2
    return jnp.concatenate([row[half:], row[:half]], axis=0)


def kernel(
    n,
    x_ref,
    gain1_ref,
    prof_ref,
    mix_ref,
    gain2_ref,
    proj_ref,
    scale_ref,
    final_ref,
    reach_ref,
    out_ref,
    xhalo,
    ext,
    taps,
    toeplitz,
    basis,
    hidden,
    att,
    queries,
    keys,
    values,
    bias,
    heads,
    mixture,
    send_x,
    recv_x,
    send_a,
    recv_a,
):
    rows, longitudes, channels = x_ref.shape
    me = lax.axis_index("band")
    has_up = me > 0
    has_down = me < n - 1
    depth = PATCH_LAT_EXTENT
    sent = longitudes + 16

    def x_copy(side):
        return pltpu.make_async_remote_copy(
            src_ref=x_ref.at[0 if side == 0 else rows - 1],
            dst_ref=xhalo.at[1 - side],
            send_sem=send_x.at[side],
            recv_sem=recv_x.at[1 - side],
            device_id={"band": me - 1 if side == 0 else me + 1},
            device_id_type=pl.DeviceIdType.MESH,
        )

    def a_copy(side, step):
        source = depth + step if side == 0 else rows + step
        target = rows + depth + step if side == 0 else step
        slot = side * depth + step
        other = (1 - side) * depth + step
        return pltpu.make_async_remote_copy(
            src_ref=att.at[source, pl.ds(0, sent)],
            dst_ref=att.at[target, pl.ds(0, sent)],
            send_sem=send_a.at[slot],
            recv_sem=recv_a.at[other],
            device_id={"band": me - 1 if side == 0 else me + 1},
            device_id_type=pl.DeviceIdType.MESH,
        )

    has = (has_up, has_down)

    barrier = pltpu.get_barrier_semaphore()
    for side in range(2):

        @pl.when(has[side])
        def _():
            pl.semaphore_signal(
                barrier,
                inc=1,
                device_id={"band": me - 1 if side == 0 else me + 1},
                device_id_type=pl.DeviceIdType.MESH,
            )

    pl.semaphore_wait(barrier, jnp.where(me == 0, 1, 2) - jnp.where(me == n - 1, 1, 0))

    for side in range(2):

        @pl.when(has[side])
        def _():
            x_copy(side).start()

    gain1 = gain1_ref[...]
    gain2 = gain2_ref[...]

    shape2 = (HEAD_COUNT * QUERY_BLOCK, channels)
    sub = lax.broadcasted_iota(jnp.int32, shape2, 0)
    lane = lax.broadcasted_iota(jnp.int32, shape2, 1)
    heads[...] = jnp.where(sub // QUERY_BLOCK == lane // HEAD_WIDTH, 1.0, 0.0).astype(BF16)
    ones_blocks = heads if QUERY_BLOCK == HEAD_WIDTH else None

    key = lax.broadcasted_iota(jnp.int32, (QUERY_BLOCK, KEYS), 1)
    query = lax.broadcasted_iota(jnp.int32, (QUERY_BLOCK, KEYS), 0)
    for r in range(rows):
        limit = jnp.zeros((QUERY_BLOCK, KEYS), jnp.int32)
        start = jnp.zeros((QUERY_BLOCK, KEYS), jnp.int32)
        for a in range(ROWS_A):
            inside = key >= a * KEY_WINDOW
            limit = jnp.where(inside, reach_ref[r, a], limit)
            start = jnp.where(inside, a * KEY_WINDOW, start)
        distance = jnp.abs(key - start - DISC_REACH - query)
        bias[r] = jnp.where(distance <= limit, 0.0, -1e30).astype(F32)

    for r in range(rows):
        ext[r + 1] = ring_pad(rms(x_ref[r].astype(F32), gain1)).astype(BF16)

    tap_lane = lax.broadcasted_iota(jnp.int32, (16, KEYS), 1)

    def build_filters(r):
        taps[...] = jnp.zeros_like(taps)
        taps[0:BASIS_COUNT, 0 : 3 * TAPS] = prof_ref[r]
        flat = taps[...]
        placed = jnp.zeros_like(flat)
        for a in range(3):
            begin = a * CONV_WINDOW + CONV_REACH
            moved = pltpu.roll(flat, begin - a * TAPS, axis=1) if begin - a * TAPS else flat
            offset = tap_lane - begin
            reach = jnp.minimum(reach_ref[r, PATCH_LAT_EXTENT - 1 + a], CONV_REACH)
            inside = jnp.abs(offset - CONV_REACH) <= reach
            placed = jnp.where(inside, moved, placed)
        for k in range(BASIS_COUNT):
            spread = jnp.broadcast_to(placed[k : k + 1], (CONV_BLOCK, KEYS))
            spread = pltpu.roll(spread, 0, axis=1, stride=1, stride_axis=0)
            toeplitz[k * CONV_BLOCK : (k + 1) * CONV_BLOCK] = spread.astype(BF16)

    def conv_row(r):
        build_filters(r)

        def conv_block(b, carry):
            at = pl.multiple_of(b * CONV_BLOCK, CONV_BLOCK)
            window = jnp.concatenate(
                [
                    ext[r, pl.ds(at, CONV_WINDOW)],
                    ext[r + 1, pl.ds(at, CONV_WINDOW)],
                    ext[r + 2, pl.ds(at, KEYS - 2 * CONV_WINDOW)],
                ],
                axis=0,
            )
            sums = jnp.dot(toeplitz[...], window, preferred_element_type=F32).astype(BF16)
            for k in range(BASIS_COUNT):
                basis[pl.ds(at, CONV_BLOCK), k * channels : (k + 1) * channels] = sums[
                    k * CONV_BLOCK : (k + 1) * CONV_BLOCK
                ]
            return carry

        lax.fori_loop(0, longitudes // CONV_BLOCK, conv_block, 0)
        mixed = jnp.dot(basis[...], mix_ref[...], preferred_element_type=F32)
        total = x_ref[r].astype(F32) + mixed
        hidden[r] = total
        normed = rms(total, gain2)
        att[r + depth] = ring_pad(normed).astype(BF16)
        queries[r] = unit(
            jnp.dot(
                normed.astype(BF16), proj_ref[:, 0:channels], preferred_element_type=F32
            )
        )

        if r < depth:

            @pl.when(has_up)
            def _():
                a_copy(0, r).start()

            if r == 0 or r == 1:

                @pl.when(jnp.logical_not(has_up))
                def _():
                    att[depth - 1 - r] = ring_pad(half_turn(normed)).astype(BF16)

        if r >= rows - depth:

            @pl.when(has_down)
            def _():
                a_copy(1, r - (rows - depth)).start()

            @pl.when(jnp.logical_not(has_down))
            def _():
                att[2 * rows + 2 * depth - 1 - (r + depth) + 0] = ring_pad(
                    half_turn(normed)
                ).astype(BF16)

    def unit(product):
        value = product.astype(BF16).astype(F32)
        square = value * value
        high = square.astype(BF16)
        low = (square - high.astype(F32)).astype(BF16)
        total = jnp.dot(high, ones_blocks[...], preferred_element_type=F32)
        total = total + jnp.dot(low, ones_blocks[...], preferred_element_type=F32)
        return (value * lax.rsqrt(total + EPSILON)).astype(BF16)

    def key_value(row):
        source = att[row]
        keys[row] = unit(
            jnp.dot(source, proj_ref[:, channels : 2 * channels], preferred_element_type=F32)
        )
        values[row] = jnp.dot(
            source, proj_ref[:, 2 * channels :], preferred_element_type=F32
        ).astype(BF16)

    att[0:depth, sent:] = jnp.zeros((depth, longitudes + PAD + TAIL - sent, channels), BF16)
    att[rows + depth :, sent:] = jnp.zeros((depth, longitudes + PAD + TAIL - sent, channels), BF16)

    for r in range(1, rows - 1):
        conv_row(r)

    for side in range(2):
        edge = 0 if side == 0 else rows - 1
        slot = 0 if side == 0 else rows + 1

        @pl.when(has[side])
        def _():
            x_copy(1 - side).wait_recv()
            ext[slot] = ring_pad(rms(xhalo[side].astype(F32), gain1)).astype(BF16)

        @pl.when(jnp.logical_not(has[side]))
        def _():
            ext[slot] = ring_pad(half_turn(rms(x_ref[edge].astype(F32), gain1))).astype(BF16)

        conv_row(edge)

    for r in range(rows):
        key_value(r + depth)

    for side in range(2):
        for step in range(depth):

            @pl.when(has[side])
            def _():
                a_copy(1 - side, step).wait_recv()

    for step in range(depth):
        key_value(step)
        key_value(rows + depth + step)

    head_lane = lax.broadcasted_iota(jnp.int32, (QUERY_BLOCK, channels), 1) // HEAD_WIDTH

    def attend(r, b):
        at = pl.multiple_of(b * QUERY_BLOCK, QUERY_BLOCK)
        probe = queries[r, pl.ds(at, QUERY_BLOCK)]
        spread = jnp.concatenate([probe] * HEAD_COUNT, axis=0) * heads[...]

        def windows(ref):
            sizes = [KEY_WINDOW] * (ROWS_A - 1) + [KEYS - (ROWS_A - 1) * KEY_WINDOW]
            return jnp.concatenate(
                [ref[r + a, pl.ds(at, sizes[a])] for a in range(ROWS_A)], axis=0
            )

        scores = lax.dot_general(
            spread, windows(keys), (((1,), (1,)), ((), ())), preferred_element_type=F32
        )
        seen = bias[r]
        parts, sums = [], []
        for h in range(HEAD_COUNT):
            part = scores[h * QUERY_BLOCK : (h + 1) * QUERY_BLOCK] + seen
            peak = jnp.max(part, axis=-1, keepdims=True)
            part = jnp.exp2((part - peak) * (scale_ref[h] * LOG2E))
            sums.append(jnp.sum(part, axis=-1, keepdims=True))
            parts.append(part.astype(BF16))
        mixed = jnp.dot(
            jnp.concatenate(parts, axis=0), windows(values), preferred_element_type=F32
        )
        result = jnp.zeros((QUERY_BLOCK, channels), F32)
        for h in range(HEAD_COUNT):
            share = mixed[h * QUERY_BLOCK : (h + 1) * QUERY_BLOCK] * (1.0 / sums[h])
            result = jnp.where(head_lane == h, share, result)
        mixture[pl.ds(at, QUERY_BLOCK)] = result.astype(BF16)

    for r in range(rows):

        def attend_block(b, carry):
            attend(r, b)
            return carry

        lax.fori_loop(0, longitudes // QUERY_BLOCK, attend_block, 0)
        out_ref[r] = (
            hidden[r] + jnp.dot(mixture[...], final_ref[...], preferred_element_type=F32)
        ).astype(BF16)

    for side in range(2):

        @pl.when(has[side])
        def _():
            x_copy(side).wait_send()
            for step in range(depth):
                a_copy(side, step).wait_send()


def on_device(
    grid_inputs,
    stencil_prenorm_scale,
    patch_kernel_profiles,
    channel_mixer_tensor,
    softmax_prenorm_scale,
    probe_lookup_content_projector,
    head_logit_scales,
    final_projector,
    azimuth_reaches,
    *,
    n,
):
    rows, longitudes, channels = grid_inputs.shape
    padded = longitudes + PAD + TAIL
    wide = rows + 2 * PATCH_LAT_EXTENT
    vmem = pl.BlockSpec(memory_space=pltpu.VMEM)
    smem = pl.BlockSpec(memory_space=pltpu.SMEM)
    return pl.pallas_call(
        functools.partial(kernel, n),
        out_shape=jax.ShapeDtypeStruct(grid_inputs.shape, BF16),
        in_specs=[vmem, vmem, vmem, vmem, vmem, vmem, smem, vmem, smem],
        out_specs=vmem,
        scratch_shapes=[
            pltpu.VMEM((2, longitudes, channels), BF16),
            pltpu.VMEM((rows + 2, padded, channels), BF16),
            pltpu.VMEM((16, KEYS), F32),
            pltpu.VMEM((BASIS_COUNT * CONV_BLOCK, KEYS), BF16),
            pltpu.VMEM((longitudes, BASIS_COUNT * channels), BF16),
            pltpu.VMEM((rows, longitudes, channels), F32),
            pltpu.VMEM((wide, padded, channels), BF16),
            pltpu.VMEM((rows, longitudes, channels), BF16),
            pltpu.VMEM((wide, padded, channels), BF16),
            pltpu.VMEM((wide, padded, channels), BF16),
            pltpu.VMEM((rows, QUERY_BLOCK, KEYS), F32),
            pltpu.VMEM((HEAD_COUNT * QUERY_BLOCK, channels), BF16),
            pltpu.VMEM((longitudes, channels), BF16),
            pltpu.SemaphoreType.DMA((2,)),
            pltpu.SemaphoreType.DMA((2,)),
            pltpu.SemaphoreType.DMA((2 * PATCH_LAT_EXTENT,)),
            pltpu.SemaphoreType.DMA((2 * PATCH_LAT_EXTENT,)),
        ],
        compiler_params=pltpu.CompilerParams(
            collective_id=0, has_side_effects=True, vmem_limit_bytes=48 * 1024 * 1024
        ),
    )(
        grid_inputs,
        stencil_prenorm_scale.reshape(1, channels),
        patch_kernel_profiles,
        channel_mixer_tensor,
        softmax_prenorm_scale.reshape(1, channels),
        probe_lookup_content_projector,
        head_logit_scales,
        final_projector,
        azimuth_reaches,
    )


def solution(mesh):
    placed = (
        P(("members", "band"), None, None),
        P(),
        P("band", None, None),
        P(),
        P(),
        P(),
        P(),
        P(),
        P("band", None),
    )
    return jax.shard_map(
        functools.partial(on_device, n=mesh.shape["band"]),
        mesh=mesh,
        in_specs=placed,
        out_specs=P(("members", "band"), None, None),
        check_vma=False,
    )
```

```python
import functools
import math

import jax
import jax.numpy as jnp
from jax import lax
from jax.experimental import pallas as pl
from jax.experimental.pallas import tpu as pltpu
from jax.sharding import PartitionSpec as P

HEAD_COUNT = 8
HEAD_WIDTH = 32
BASIS_COUNT = 9
CONV_REACH = 4
PATCH_LAT_EXTENT = 2
DISC_REACH = 8
EPSILON = 1e-06

TAPS = 2 * CONV_REACH + 1
CONV_BLOCK = 64
CONV_WINDOW = CONV_BLOCK + 16
QUERY_BLOCK = 32
KEY_WINDOW = QUERY_BLOCK + 2 * DISC_REACH
KEYS = 256
GROUP = 4
ROWS_A = 2 * PATCH_LAT_EXTENT + 1
PAD = DISC_REACH
TAIL = 24
LOG2E = math.log2(math.e)
F32 = jnp.float32
BF16 = jnp.bfloat16


def rms(values, gain):
    inverse = lax.rsqrt(jnp.mean(values * values, axis=-1, keepdims=True) + EPSILON)
    return values * inverse * gain


def ring_pad(row):
    return jnp.concatenate([row[-PAD:], row, row[:TAIL]], axis=0)


def half_turn(row):
    half = row.shape[0] // 2
    return jnp.concatenate([row[half:], row[:half]], axis=0)


def kernel(
    n,
    x_hbm,
    gain1_hbm,
    prof_hbm,
    mix_hbm,
    gain2_hbm,
    proj_hbm,
    scale_hbm,
    final_hbm,
    reach_hbm,
    out_ref,
    x_ref,
    gain1_ref,
    prof_ref,
    mix_ref,
    gain2_ref,
    proj_ref,
    scale_ref,
    final_ref,
    reach_ref,
    xhalo,
    ext,
    taps,
    toeplitz,
    basis,
    hidden,
    att,
    queries,
    keys,
    values,
    bias,
    heads,
    mixture,
    send_x,
    recv_x,
    send_a,
    recv_a,
    loads,
):
    rows, longitudes, channels = x_ref.shape
    me = lax.axis_index("band")
    has_up = me > 0
    has_down = me < n - 1
    depth = PATCH_LAT_EXTENT
    sent = longitudes + 16

    def x_copy(side):
        return pltpu.make_async_remote_copy(
            src_ref=x_hbm.at[0 if side == 0 else rows - 1],
            dst_ref=xhalo.at[1 - side],
            send_sem=send_x.at[side],
            recv_sem=recv_x.at[1 - side],
            device_id={"band": me - 1 if side == 0 else me + 1},
            device_id_type=pl.DeviceIdType.MESH,
        )

    def a_copy(side, step):
        source = depth + step if side == 0 else rows + step
        target = rows + depth + step if side == 0 else step
        slot = side * depth + step
        other = (1 - side) * depth + step
        return pltpu.make_async_remote_copy(
            src_ref=att.at[source, pl.ds(0, sent)],
            dst_ref=att.at[target, pl.ds(0, sent)],
            send_sem=send_a.at[slot],
            recv_sem=recv_a.at[other],
            device_id={"band": me - 1 if side == 0 else me + 1},
            device_id_type=pl.DeviceIdType.MESH,
        )

    has = (has_up, has_down)

    pairs = (
        (x_hbm, x_ref),
        (gain1_hbm, gain1_ref),
        (reach_hbm, reach_ref),
        (prof_hbm, prof_ref),
        (mix_hbm, mix_ref),
        (gain2_hbm, gain2_ref),
        (proj_hbm, proj_ref),
        (scale_hbm, scale_ref),
        (final_hbm, final_ref),
    )
    fetch = [
        pltpu.make_async_copy(source, target, loads.at[i])
        for i, (source, target) in enumerate(pairs)
    ]
    for copy in fetch:
        copy.start()

    barrier = pltpu.get_barrier_semaphore()
    for side in range(2):

        @pl.when(has[side])
        def _():
            pl.semaphore_signal(
                barrier,
                inc=1,
                device_id={"band": me - 1 if side == 0 else me + 1},
                device_id_type=pl.DeviceIdType.MESH,
            )

    pl.semaphore_wait(barrier, jnp.where(me == 0, 1, 2) - jnp.where(me == n - 1, 1, 0))

    for side in range(2):

        @pl.when(has[side])
        def _():
            x_copy(side).start()

    shape2 = (HEAD_COUNT * QUERY_BLOCK, channels)
    sub = lax.broadcasted_iota(jnp.int32, shape2, 0)
    lane = lax.broadcasted_iota(jnp.int32, shape2, 1)
    heads[...] = jnp.where(sub // QUERY_BLOCK == lane // HEAD_WIDTH, 1.0, 0.0).astype(BF16)
    ones_blocks = heads if QUERY_BLOCK == HEAD_WIDTH else None

    key = lax.broadcasted_iota(jnp.int32, (QUERY_BLOCK, KEYS), 1)
    query = lax.broadcasted_iota(jnp.int32, (QUERY_BLOCK, KEYS), 0)
    fetch[2].wait()
    for r in range(rows):
        limit = jnp.zeros((QUERY_BLOCK, KEYS), jnp.int32)
        start = jnp.zeros((QUERY_BLOCK, KEYS), jnp.int32)
        for a in range(ROWS_A):
            inside = key >= a * KEY_WINDOW
            limit = jnp.where(inside, reach_ref[r, a], limit)
            start = jnp.where(inside, a * KEY_WINDOW, start)
        distance = jnp.abs(key - start - DISC_REACH - query)
        bias[r] = jnp.where(distance <= limit, 0.0, -1e30).astype(F32)

    fetch[0].wait()
    fetch[1].wait()
    gain1 = gain1_ref[...]

    for r in range(rows):
        ext[r + 1] = ring_pad(rms(x_ref[r].astype(F32), gain1)).astype(BF16)

    tap_lane = lax.broadcasted_iota(jnp.int32, (16, KEYS), 1)

    def build_filters(r):
        taps[...] = jnp.zeros_like(taps)
        taps[0:BASIS_COUNT, 0 : 3 * TAPS] = prof_ref[:, r, :]
        flat = taps[...]
        placed = jnp.zeros_like(flat)
        for a in range(3):
            begin = a * CONV_WINDOW + CONV_REACH
            moved = pltpu.roll(flat, begin - a * TAPS, axis=1) if begin - a * TAPS else flat
            offset = tap_lane - begin
            reach = jnp.minimum(reach_ref[r, PATCH_LAT_EXTENT - 1 + a], CONV_REACH)
            inside = jnp.abs(offset - CONV_REACH) <= reach
            placed = jnp.where(inside, moved, placed)
        for k in range(BASIS_COUNT):
            spread = jnp.broadcast_to(placed[k : k + 1], (CONV_BLOCK, KEYS))
            spread = pltpu.roll(spread, 0, axis=1, stride=1, stride_axis=0)
            toeplitz[k * CONV_BLOCK : (k + 1) * CONV_BLOCK] = spread.astype(BF16)

    fetch[3].wait()

    def conv_row(r, first=False):
        build_filters(r)

        def conv_block(b, carry):
            at = pl.multiple_of(b * CONV_BLOCK, CONV_BLOCK)
            window = jnp.concatenate(
                [
                    ext[r, pl.ds(at, CONV_WINDOW)],
                    ext[r + 1, pl.ds(at, CONV_WINDOW)],
                    ext[r + 2, pl.ds(at, KEYS - 2 * CONV_WINDOW)],
                ],
                axis=0,
            )
            sums = jnp.dot(toeplitz[...], window, preferred_element_type=F32).astype(BF16)
            for k in range(BASIS_COUNT):
                basis[pl.ds(at, CONV_BLOCK), k * channels : (k + 1) * channels] = sums[
                    k * CONV_BLOCK : (k + 1) * CONV_BLOCK
                ]
            return carry

        lax.fori_loop(0, longitudes // CONV_BLOCK, conv_block, 0, unroll=2)
        if first:
            fetch[4].wait()
            fetch[5].wait()
            fetch[6].wait()
        gain2 = gain2_ref[...]
        mixed = jnp.dot(basis[...], mix_ref[...], preferred_element_type=F32)
        total = x_ref[r].astype(F32) + mixed
        hidden[r] = total
        normed = rms(total, gain2)
        att[r + depth] = ring_pad(normed).astype(BF16)
        queries[r] = unit(
            jnp.dot(
                normed.astype(BF16), proj_ref[:, 0:channels], preferred_element_type=F32
            )
        )

        if r < depth:

            @pl.when(has_up)
            def _():
                a_copy(0, r).start()

            if r == 0 or r == 1:

                @pl.when(jnp.logical_not(has_up))
                def _():
                    att[depth - 1 - r] = ring_pad(half_turn(normed)).astype(BF16)

        if r >= rows - depth:

            @pl.when(has_down)
            def _():
                a_copy(1, r - (rows - depth)).start()

            @pl.when(jnp.logical_not(has_down))
            def _():
                att[2 * rows + 2 * depth - 1 - (r + depth) + 0] = ring_pad(
                    half_turn(normed)
                ).astype(BF16)

    def unit(product):
        value = product.astype(BF16).astype(F32)
        square = value * value
        high = square.astype(BF16)
        low = (square - high.astype(F32)).astype(BF16)
        total = jnp.dot(high, ones_blocks[...], preferred_element_type=F32)
        total = total + jnp.dot(low, ones_blocks[...], preferred_element_type=F32)
        return (value * lax.rsqrt(total + EPSILON)).astype(BF16)

    def key_value(row):
        source = att[row]
        keys[row] = unit(
            jnp.dot(source, proj_ref[:, channels : 2 * channels], preferred_element_type=F32)
        )
        values[row] = jnp.dot(
            source, proj_ref[:, 2 * channels :], preferred_element_type=F32
        ).astype(BF16)

    att[0:depth, sent:] = jnp.zeros((depth, longitudes + PAD + TAIL - sent, channels), BF16)
    att[rows + depth :, sent:] = jnp.zeros((depth, longitudes + PAD + TAIL - sent, channels), BF16)

    def edge_row(side):
        edge = 0 if side == 0 else rows - 1
        slot = 0 if side == 0 else rows + 1

        @pl.when(has[side])
        def _():
            x_copy(1 - side).wait_recv()
            ext[slot] = ring_pad(rms(xhalo[side].astype(F32), gain1)).astype(BF16)

        @pl.when(jnp.logical_not(has[side]))
        def _():
            ext[slot] = ring_pad(half_turn(rms(x_ref[edge].astype(F32), gain1))).astype(BF16)

    if rows == 2:
        edge_row(1)
    for r in range(1, rows - 1):
        conv_row(r, r == 1)
    if rows > 2:
        edge_row(1)
    conv_row(rows - 1, rows == 2)
    edge_row(0)
    conv_row(0)

    for r in range(rows):
        key_value(r + depth)
    fetch[7].wait()
    fetch[8].wait()

    def halo_rows(side):
        for step in range(depth):

            @pl.when(has[side])
            def _():
                a_copy(1 - side, step).wait_recv()

        for step in range(depth):
            key_value(step if side == 0 else rows + depth + step)

    head_lane = lax.broadcasted_iota(jnp.int32, (QUERY_BLOCK, channels), 1) // HEAD_WIDTH
    sizes = [KEY_WINDOW] * (ROWS_A - 1) + [KEYS - (ROWS_A - 1) * KEY_WINDOW]

    def attend(r, starts):
        def windows(ref, at):
            return jnp.concatenate(
                [ref[r + a, pl.ds(at, sizes[a])] for a in range(ROWS_A)], axis=0
            )

        seen = bias[r]
        all_scores = []
        for at in starts:
            probe = queries[r, pl.ds(at, QUERY_BLOCK)]
            spread = jnp.concatenate([probe] * HEAD_COUNT, axis=0) * heads[...]
            all_scores.append(
                lax.dot_general(
                    spread,
                    windows(keys, at),
                    (((1,), (1,)), ((), ())),
                    preferred_element_type=F32,
                )
            )
        all_mixed, all_sums = [], []
        for at, scores in zip(starts, all_scores):
            parts, sums = [], []
            for h in range(HEAD_COUNT):
                part = scores[h * QUERY_BLOCK : (h + 1) * QUERY_BLOCK] + seen
                peak = jnp.max(part, axis=-1, keepdims=True)
                part = jnp.exp2((part - peak) * (scale_ref[h] * LOG2E))
                sums.append(jnp.sum(part, axis=-1, keepdims=True))
                parts.append(part.astype(BF16))
            all_mixed.append(
                jnp.dot(
                    jnp.concatenate(parts, axis=0),
                    windows(values, at),
                    preferred_element_type=F32,
                )
            )
            all_sums.append(sums)
        for at, mixed, sums in zip(starts, all_mixed, all_sums):
            result = jnp.zeros((QUERY_BLOCK, channels), F32)
            for h in range(HEAD_COUNT):
                share = mixed[h * QUERY_BLOCK : (h + 1) * QUERY_BLOCK] * (1.0 / sums[h])
                result = jnp.where(head_lane == h, share, result)
            mixture[pl.ds(at, QUERY_BLOCK)] = result.astype(BF16)

    group = GROUP
    while longitudes % (group * QUERY_BLOCK):
        group -= 1

    def attend_row(r):
        def attend_group(b, carry):
            at = pl.multiple_of(b * (group * QUERY_BLOCK), QUERY_BLOCK)
            attend(r, [at + g * QUERY_BLOCK for g in range(group)])
            return carry

        lax.fori_loop(0, longitudes // (group * QUERY_BLOCK), attend_group, 0)
        out_ref[r] = (
            hidden[r] + jnp.dot(mixture[...], final_ref[...], preferred_element_type=F32)
        ).astype(BF16)

    halo_rows(0)
    early = max(rows - depth, 0)
    for r in range(early):
        attend_row(r)
    halo_rows(1)
    for r in range(early, rows):
        attend_row(r)

    for side in range(2):

        @pl.when(has[side])
        def _():
            x_copy(side).wait_send()
            for step in range(depth):
                a_copy(side, step).wait_send()


def on_device(
    grid_inputs,
    stencil_prenorm_scale,
    patch_kernel_profiles,
    channel_mixer_tensor,
    softmax_prenorm_scale,
    probe_lookup_content_projector,
    head_logit_scales,
    final_projector,
    azimuth_reaches,
    *,
    n,
):
    rows, longitudes, channels = grid_inputs.shape
    padded = longitudes + PAD + TAIL
    wide = rows + 2 * PATCH_LAT_EXTENT
    vmem = pl.BlockSpec(memory_space=pltpu.VMEM)
    hbm = pl.BlockSpec(memory_space=pltpu.HBM)
    return pl.pallas_call(
        functools.partial(kernel, n),
        out_shape=jax.ShapeDtypeStruct(grid_inputs.shape, BF16),
        in_specs=[hbm] * 9,
        out_specs=vmem,
        scratch_shapes=[
            pltpu.VMEM(grid_inputs.shape, BF16),
            pltpu.VMEM((1, channels), F32),
            pltpu.VMEM((patch_kernel_profiles.shape[1], rows, 3 * TAPS), F32),
            pltpu.VMEM(channel_mixer_tensor.shape, BF16),
            pltpu.VMEM((1, channels), F32),
            pltpu.VMEM(probe_lookup_content_projector.shape, BF16),
            pltpu.SMEM(head_logit_scales.shape, F32),
            pltpu.VMEM(final_projector.shape, BF16),
            pltpu.SMEM(azimuth_reaches.shape, jnp.int32),
            pltpu.VMEM((2, longitudes, channels), BF16),
            pltpu.VMEM((rows + 2, padded, channels), BF16),
            pltpu.VMEM((16, KEYS), F32),
            pltpu.VMEM((BASIS_COUNT * CONV_BLOCK, KEYS), BF16),
            pltpu.VMEM((longitudes, BASIS_COUNT * channels), BF16),
            pltpu.VMEM((rows, longitudes, channels), F32),
            pltpu.VMEM((wide, padded, channels), BF16),
            pltpu.VMEM((rows, longitudes, channels), BF16),
            pltpu.VMEM((wide, padded, channels), BF16),
            pltpu.VMEM((wide, padded, channels), BF16),
            pltpu.VMEM((rows, QUERY_BLOCK, KEYS), F32),
            pltpu.VMEM((HEAD_COUNT * QUERY_BLOCK, channels), BF16),
            pltpu.VMEM((longitudes, channels), BF16),
            pltpu.SemaphoreType.DMA((2,)),
            pltpu.SemaphoreType.DMA((2,)),
            pltpu.SemaphoreType.DMA((2 * PATCH_LAT_EXTENT,)),
            pltpu.SemaphoreType.DMA((2 * PATCH_LAT_EXTENT,)),
            pltpu.SemaphoreType.DMA((9,)),
        ],
        compiler_params=pltpu.CompilerParams(
            collective_id=0, has_side_effects=True, vmem_limit_bytes=64 * 1024 * 1024
        ),
    )(
        grid_inputs,
        stencil_prenorm_scale.reshape(1, channels),
        patch_kernel_profiles.transpose(1, 0, 2),
        channel_mixer_tensor,
        softmax_prenorm_scale.reshape(1, channels),
        probe_lookup_content_projector,
        head_logit_scales,
        final_projector,
        azimuth_reaches,
    )


def solution(mesh):
    placed = (
        P(("members", "band"), None, None),
        P(),
        P("band", None, None),
        P(),
        P(),
        P(),
        P(),
        P(),
        P("band", None),
    )
    return jax.shard_map(
        functools.partial(on_device, n=mesh.shape["band"]),
        mesh=mesh,
        in_specs=placed,
        out_specs=P(("members", "band"), None, None),
        check_vma=False,
    )
```

```python
import functools
import math

import jax
import jax.numpy as jnp
from jax import lax
from jax.experimental import pallas as pl
from jax.experimental.pallas import tpu as pltpu
from jax.sharding import PartitionSpec as P

HEAD_COUNT = 8
HEAD_WIDTH = 32
BASIS_COUNT = 9
CONV_REACH = 4
PATCH_LAT_EXTENT = 2
DISC_REACH = 8
EPSILON = 1e-06

TAPS = 2 * CONV_REACH + 1
CONV_BLOCK = 64
CONV_WINDOW = CONV_BLOCK + 16
QUERY_BLOCK = 32
KEY_WINDOW = QUERY_BLOCK + 2 * DISC_REACH
KEYS = 256
GROUP = 4
ROWS_A = 2 * PATCH_LAT_EXTENT + 1
PAD = DISC_REACH
TAIL = 24
LOG2E = math.log2(math.e)
F32 = jnp.float32
BF16 = jnp.bfloat16


def rms(values, gain):
    inverse = lax.rsqrt(jnp.mean(values * values, axis=-1, keepdims=True) + EPSILON)
    return values * inverse * gain


def ring_pad(row):
    return jnp.concatenate([row[-PAD:], row, row[:TAIL]], axis=0)


def half_turn(row):
    half = row.shape[0] // 2
    return jnp.concatenate([row[half:], row[:half]], axis=0)


def kernel(
    n,
    x_hbm,
    gain1_hbm,
    prof_hbm,
    mix_hbm,
    gain2_hbm,
    proj_hbm,
    scale_hbm,
    final_hbm,
    reach_hbm,
    out_ref,
    x_ref,
    gain1_ref,
    prof_ref,
    mix_ref,
    gain2_ref,
    proj_ref,
    scale_ref,
    final_ref,
    reach_ref,
    xhalo,
    ext,
    taps,
    toeplitz,
    basis,
    hidden,
    att,
    queries,
    keys,
    values,
    bias,
    heads,
    mixture,
    send_x,
    recv_x,
    send_a,
    recv_a,
    loads,
):
    rows, longitudes, channels = x_ref.shape
    assert rows > PATCH_LAT_EXTENT
    me = lax.axis_index("band")
    depth = PATCH_LAT_EXTENT
    sent = longitudes + 16
    far = lax.rem(me, 2)
    near = 1 - far

    def present(side):
        other = me + 2 * side - 1
        return jnp.logical_and(other >= 0, other < n)

    def x_copy(side):
        return pltpu.make_async_remote_copy(
            src_ref=x_hbm.at[side * (rows - 1)],
            dst_ref=xhalo.at[1 - side],
            send_sem=send_x.at[side],
            recv_sem=recv_x.at[1 - side],
            device_id={"band": me + 2 * side - 1},
            device_id_type=pl.DeviceIdType.MESH,
        )

    def a_copy(side, step):
        source = (1 - side) * depth + side * rows + step
        target = (1 - side) * (rows + depth) + step
        return pltpu.make_async_remote_copy(
            src_ref=att.at[source, pl.ds(0, sent)],
            dst_ref=att.at[target, pl.ds(0, sent)],
            send_sem=send_a.at[side * depth + step],
            recv_sem=recv_a.at[(1 - side) * depth + step],
            device_id={"band": me + 2 * side - 1},
            device_id_type=pl.DeviceIdType.MESH,
        )

    pairs = (
        (x_hbm, x_ref),
        (gain1_hbm, gain1_ref),
        (reach_hbm, reach_ref),
        (prof_hbm, prof_ref),
        (mix_hbm, mix_ref),
        (gain2_hbm, gain2_ref),
        (proj_hbm, proj_ref),
        (scale_hbm, scale_ref),
        (final_hbm, final_ref),
    )
    fetch = [
        pltpu.make_async_copy(source, target, loads.at[i])
        for i, (source, target) in enumerate(pairs)
    ]
    for copy in fetch:
        copy.start()

    barrier = pltpu.get_barrier_semaphore()
    for side in range(2):

        @pl.when(present(side))
        def _():
            pl.semaphore_signal(
                barrier,
                inc=1,
                device_id={"band": me - 1 if side == 0 else me + 1},
                device_id_type=pl.DeviceIdType.MESH,
            )

    pl.semaphore_wait(barrier, jnp.where(me == 0, 1, 2) - jnp.where(me == n - 1, 1, 0))

    for side in range(2):

        @pl.when(present(side))
        def _():
            x_copy(side).start()

    shape2 = (HEAD_COUNT * QUERY_BLOCK, channels)
    sub = lax.broadcasted_iota(jnp.int32, shape2, 0)
    lane = lax.broadcasted_iota(jnp.int32, shape2, 1)
    heads[...] = jnp.where(sub // QUERY_BLOCK == lane // HEAD_WIDTH, 1.0, 0.0).astype(BF16)
    ones_blocks = heads if QUERY_BLOCK == HEAD_WIDTH else None

    key = lax.broadcasted_iota(jnp.int32, (QUERY_BLOCK, KEYS), 1)
    query = lax.broadcasted_iota(jnp.int32, (QUERY_BLOCK, KEYS), 0)
    fetch[2].wait()
    for r in range(rows):
        limit = jnp.zeros((QUERY_BLOCK, KEYS), jnp.int32)
        start = jnp.zeros((QUERY_BLOCK, KEYS), jnp.int32)
        for a in range(ROWS_A):
            inside = key >= a * KEY_WINDOW
            limit = jnp.where(inside, reach_ref[r, a], limit)
            start = jnp.where(inside, a * KEY_WINDOW, start)
        distance = jnp.abs(key - start - DISC_REACH - query)
        bias[r] = jnp.where(distance <= limit, 0.0, -1e30).astype(F32)

    fetch[0].wait()
    fetch[1].wait()
    gain1 = gain1_ref[...]

    for r in range(rows):
        ext[r + 1] = ring_pad(rms(x_ref[r].astype(F32), gain1)).astype(BF16)

    tap_lane = lax.broadcasted_iota(jnp.int32, (16, KEYS), 1)

    def build_filters(r):
        taps[...] = jnp.zeros_like(taps)
        taps[0:BASIS_COUNT, 0 : 3 * TAPS] = prof_ref[:, r, :]
        flat = taps[...]
        placed = jnp.zeros_like(flat)
        for a in range(3):
            begin = a * CONV_WINDOW + CONV_REACH
            moved = pltpu.roll(flat, begin - a * TAPS, axis=1) if begin - a * TAPS else flat
            offset = tap_lane - begin
            reach = jnp.minimum(reach_ref[r, PATCH_LAT_EXTENT - 1 + a], CONV_REACH)
            inside = jnp.abs(offset - CONV_REACH) <= reach
            placed = jnp.where(inside, moved, placed)
        for k in range(BASIS_COUNT):
            spread = jnp.broadcast_to(placed[k : k + 1], (CONV_BLOCK, KEYS))
            spread = pltpu.roll(spread, 0, axis=1, stride=1, stride_axis=0)
            toeplitz[k * CONV_BLOCK : (k + 1) * CONV_BLOCK] = spread.astype(BF16)

    fetch[3].wait()

    def conv_row(r, first=False, edge=None):
        build_filters(r)

        def conv_block(b, carry):
            at = pl.multiple_of(b * CONV_BLOCK, CONV_BLOCK)
            window = jnp.concatenate(
                [
                    ext[r, pl.ds(at, CONV_WINDOW)],
                    ext[r + 1, pl.ds(at, CONV_WINDOW)],
                    ext[r + 2, pl.ds(at, KEYS - 2 * CONV_WINDOW)],
                ],
                axis=0,
            )
            sums = jnp.dot(toeplitz[...], window, preferred_element_type=F32).astype(BF16)
            for k in range(BASIS_COUNT):
                basis[pl.ds(at, CONV_BLOCK), k * channels : (k + 1) * channels] = sums[
                    k * CONV_BLOCK : (k + 1) * CONV_BLOCK
                ]
            return carry

        lax.fori_loop(0, longitudes // CONV_BLOCK, conv_block, 0, unroll=2)
        if first:
            fetch[4].wait()
            fetch[5].wait()
            fetch[6].wait()
        gain2 = gain2_ref[...]
        mixed = jnp.dot(basis[...], mix_ref[...], preferred_element_type=F32)
        total = x_ref[r].astype(F32) + mixed
        hidden[r] = total
        normed = rms(total, gain2)
        att[r + depth] = ring_pad(normed).astype(BF16)
        queries[r] = unit(
            jnp.dot(
                normed.astype(BF16), proj_ref[:, 0:channels], preferred_element_type=F32
            )
        )

        def share(side, step, pole_slot):
            @pl.when(present(side))
            def _():
                a_copy(side, step).start()

            @pl.when(jnp.logical_not(present(side)))
            def _():
                att[pole_slot] = ring_pad(half_turn(normed)).astype(BF16)

        if edge is not None:
            share(edge, edge * (depth - 1), (1 - edge) * (depth - 1) + edge * (rows + depth))
        else:
            if r < depth:
                share(0, r, depth - 1 - r)
            if r >= rows - depth:
                share(1, r - (rows - depth), 2 * rows + depth - 1 - r)

    def unit(product):
        value = product.astype(BF16).astype(F32)
        square = value * value
        high = square.astype(BF16)
        low = (square - high.astype(F32)).astype(BF16)
        total = jnp.dot(high, ones_blocks[...], preferred_element_type=F32)
        total = total + jnp.dot(low, ones_blocks[...], preferred_element_type=F32)
        return (value * lax.rsqrt(total + EPSILON)).astype(BF16)

    def key_value(row):
        source = att[row]
        keys[row] = unit(
            jnp.dot(source, proj_ref[:, channels : 2 * channels], preferred_element_type=F32)
        )
        values[row] = jnp.dot(
            source, proj_ref[:, 2 * channels :], preferred_element_type=F32
        ).astype(BF16)

    att[0:depth, sent:] = jnp.zeros((depth, longitudes + PAD + TAIL - sent, channels), BF16)
    att[rows + depth :, sent:] = jnp.zeros((depth, longitudes + PAD + TAIL - sent, channels), BF16)

    def edge_row(side):
        row = side * (rows - 1)
        slot = side * (rows + 1)

        @pl.when(present(side))
        def _():
            x_copy(1 - side).wait_recv()
            ext[slot] = ring_pad(rms(xhalo[side].astype(F32), gain1)).astype(BF16)

        @pl.when(jnp.logical_not(present(side)))
        def _():
            ext[slot] = ring_pad(half_turn(rms(x_ref[row].astype(F32), gain1))).astype(BF16)

        conv_row(row, edge=side)

    for r in range(1, rows - 1):
        conv_row(r, r == 1)
    edge_row(far)
    edge_row(near)

    for r in range(rows):
        key_value(r + depth)
    fetch[7].wait()
    fetch[8].wait()

    def halo_rows(side):
        for step in range(depth):

            @pl.when(present(side))
            def _():
                a_copy(1 - side, step).wait_recv()

        for step in range(depth):
            key_value(side * (rows + depth) + step)

    head_lane = lax.broadcasted_iota(jnp.int32, (QUERY_BLOCK, channels), 1) // HEAD_WIDTH
    sizes = [KEY_WINDOW] * (ROWS_A - 1) + [KEYS - (ROWS_A - 1) * KEY_WINDOW]

    def attend(r, starts):
        def windows(ref, at):
            return jnp.concatenate(
                [ref[r + a, pl.ds(at, sizes[a])] for a in range(ROWS_A)], axis=0
            )

        seen = bias[r]
        all_scores = []
        for at in starts:
            probe = queries[r, pl.ds(at, QUERY_BLOCK)]
            spread = jnp.concatenate([probe] * HEAD_COUNT, axis=0) * heads[...]
            all_scores.append(
                lax.dot_general(
                    spread,
                    windows(keys, at),
                    (((1,), (1,)), ((), ())),
                    preferred_element_type=F32,
                )
            )
        all_mixed, all_sums = [], []
        for at, scores in zip(starts, all_scores):
            parts, sums = [], []
            for h in range(HEAD_COUNT):
                part = scores[h * QUERY_BLOCK : (h + 1) * QUERY_BLOCK] + seen
                peak = jnp.max(part, axis=-1, keepdims=True)
                part = jnp.exp2((part - peak) * (scale_ref[h] * LOG2E))
                sums.append(jnp.sum(part, axis=-1, keepdims=True))
                parts.append(part.astype(BF16))
            all_mixed.append(
                jnp.dot(
                    jnp.concatenate(parts, axis=0),
                    windows(values, at),
                    preferred_element_type=F32,
                )
            )
            all_sums.append(sums)
        for at, mixed, sums in zip(starts, all_mixed, all_sums):
            result = jnp.zeros((QUERY_BLOCK, channels), F32)
            for h in range(HEAD_COUNT):
                share = mixed[h * QUERY_BLOCK : (h + 1) * QUERY_BLOCK] * (1.0 / sums[h])
                result = jnp.where(head_lane == h, share, result)
            mixture[pl.ds(at, QUERY_BLOCK)] = result.astype(BF16)

    group = GROUP
    while longitudes % (group * QUERY_BLOCK):
        group -= 1

    def attend_row(r):
        def attend_group(b, carry):
            at = pl.multiple_of(b * (group * QUERY_BLOCK), QUERY_BLOCK)
            attend(r, [at + g * QUERY_BLOCK for g in range(group)])
            return carry

        lax.fori_loop(0, longitudes // (group * QUERY_BLOCK), attend_group, 0)
        out_ref[r] = (
            hidden[r] + jnp.dot(mixture[...], final_ref[...], preferred_element_type=F32)
        ).astype(BF16)

    halo_rows(near)
    attend_row(near * (rows - 1))
    halo_rows(far)
    for r in range(1, rows - 1):
        attend_row(r)
    attend_row(far * (rows - 1))

    for side in range(2):

        @pl.when(present(side))
        def _():
            x_copy(side).wait_send()
            for step in range(depth):
                a_copy(side, step).wait_send()


def on_device(
    grid_inputs,
    stencil_prenorm_scale,
    patch_kernel_profiles,
    channel_mixer_tensor,
    softmax_prenorm_scale,
    probe_lookup_content_projector,
    head_logit_scales,
    final_projector,
    azimuth_reaches,
    *,
    n,
):
    rows, longitudes, channels = grid_inputs.shape
    padded = longitudes + PAD + TAIL
    wide = rows + 2 * PATCH_LAT_EXTENT
    vmem = pl.BlockSpec(memory_space=pltpu.VMEM)
    hbm = pl.BlockSpec(memory_space=pltpu.HBM)
    return pl.pallas_call(
        functools.partial(kernel, n),
        out_shape=pltpu.VMEM(grid_inputs.shape, BF16),
        in_specs=[hbm] * 9,
        out_specs=vmem,
        scratch_shapes=[
            pltpu.VMEM(grid_inputs.shape, BF16),
            pltpu.VMEM((1, channels), F32),
            pltpu.VMEM((patch_kernel_profiles.shape[1], rows, 3 * TAPS), F32),
            pltpu.VMEM(channel_mixer_tensor.shape, BF16),
            pltpu.VMEM((1, channels), F32),
            pltpu.VMEM(probe_lookup_content_projector.shape, BF16),
            pltpu.SMEM(head_logit_scales.shape, F32),
            pltpu.VMEM(final_projector.shape, BF16),
            pltpu.SMEM(azimuth_reaches.shape, jnp.int32),
            pltpu.VMEM((2, longitudes, channels), BF16),
            pltpu.VMEM((rows + 2, padded, channels), BF16),
            pltpu.VMEM((16, KEYS), F32),
            pltpu.VMEM((BASIS_COUNT * CONV_BLOCK, KEYS), BF16),
            pltpu.VMEM((longitudes, BASIS_COUNT * channels), BF16),
            pltpu.VMEM((rows, longitudes, channels), F32),
            pltpu.VMEM((wide, padded, channels), BF16),
            pltpu.VMEM((rows, longitudes, channels), BF16),
            pltpu.VMEM((wide, padded, channels), BF16),
            pltpu.VMEM((wide, padded, channels), BF16),
            pltpu.VMEM((rows, QUERY_BLOCK, KEYS), F32),
            pltpu.VMEM((HEAD_COUNT * QUERY_BLOCK, channels), BF16),
            pltpu.VMEM((longitudes, channels), BF16),
            pltpu.SemaphoreType.DMA((2,)),
            pltpu.SemaphoreType.DMA((2,)),
            pltpu.SemaphoreType.DMA((2 * PATCH_LAT_EXTENT,)),
            pltpu.SemaphoreType.DMA((2 * PATCH_LAT_EXTENT,)),
            pltpu.SemaphoreType.DMA((9,)),
        ],
        compiler_params=pltpu.CompilerParams(
            collective_id=0, has_side_effects=True, vmem_limit_bytes=62 * 1024 * 1024
        ),
    )(
        grid_inputs,
        stencil_prenorm_scale.reshape(1, channels),
        patch_kernel_profiles.transpose(1, 0, 2),
        channel_mixer_tensor,
        softmax_prenorm_scale.reshape(1, channels),
        probe_lookup_content_projector,
        head_logit_scales,
        final_projector,
        azimuth_reaches,
    )


def solution(mesh):
    placed = (
        P(("members", "band"), None, None),
        P(),
        P("band", None, None),
        P(),
        P(),
        P(),
        P(),
        P(),
        P("band", None),
    )
    return jax.shard_map(
        functools.partial(on_device, n=mesh.shape["band"]),
        mesh=mesh,
        in_specs=placed,
        out_specs=P(("members", "band"), None, None),
        check_vma=False,
    )
```

```python
import functools
import math

import jax
import jax.numpy as jnp
from jax import lax
from jax.experimental import pallas as pl
from jax.experimental.pallas import tpu as pltpu
from jax.sharding import PartitionSpec as P

HEAD_COUNT = 8
HEAD_WIDTH = 32
BASIS_COUNT = 9
CONV_REACH = 4
PATCH_LAT_EXTENT = 2
DISC_REACH = 8
EPSILON = 1e-06

TAPS = 2 * CONV_REACH + 1
CONV_BLOCK = 64
CONV_WINDOW = CONV_BLOCK + 16
QUERY_BLOCK = 32
KEY_WINDOW = QUERY_BLOCK + 2 * DISC_REACH
KEYS = 256
GROUP = 6
ROWS_A = 2 * PATCH_LAT_EXTENT + 1
PAD = DISC_REACH
TAIL = 24
LOG2E = math.log2(math.e)
F32 = jnp.float32
BF16 = jnp.bfloat16


def rms(values, gain):
    inverse = lax.rsqrt(jnp.mean(values * values, axis=-1, keepdims=True) + EPSILON)
    return values * inverse * gain


def ring_pad(row):
    return jnp.concatenate([row[-PAD:], row, row[:TAIL]], axis=0)


def half_turn(row):
    half = row.shape[0] // 2
    return jnp.concatenate([row[half:], row[:half]], axis=0)


def kernel(
    n,
    x_hbm,
    gain1_hbm,
    prof_hbm,
    mix_hbm,
    gain2_hbm,
    proj_hbm,
    scale_hbm,
    final_hbm,
    reach_hbm,
    out_ref,
    x_ref,
    gain1_ref,
    prof_ref,
    mix_ref,
    gain2_ref,
    proj_ref,
    scale_ref,
    final_ref,
    reach_ref,
    xhalo,
    ext,
    taps,
    toeplitz,
    basis,
    hidden,
    att,
    queries,
    keys,
    values,
    bias,
    heads,
    mixture,
    send_x,
    recv_x,
    send_a,
    recv_a,
    loads,
):
    rows, longitudes, channels = x_ref.shape
    assert rows > PATCH_LAT_EXTENT
    me = lax.axis_index("band")
    depth = PATCH_LAT_EXTENT
    sent = longitudes
    far = lax.rem(me, 2)
    near = 1 - far

    def present(side):
        other = me + 2 * side - 1
        return jnp.logical_and(other >= 0, other < n)

    def x_copy(side):
        return pltpu.make_async_remote_copy(
            src_ref=x_hbm.at[side * (rows - 1)],
            dst_ref=xhalo.at[1 - side],
            send_sem=send_x.at[side],
            recv_sem=recv_x.at[1 - side],
            device_id={"band": me + 2 * side - 1},
            device_id_type=pl.DeviceIdType.MESH,
        )

    def a_copy(side, step):
        source = (1 - side) * depth + side * rows + step
        target = (1 - side) * (rows + depth) + step
        return pltpu.make_async_remote_copy(
            src_ref=att.at[source, pl.ds(0, sent)],
            dst_ref=att.at[target, pl.ds(0, sent)],
            send_sem=send_a.at[side * depth + step],
            recv_sem=recv_a.at[(1 - side) * depth + step],
            device_id={"band": me + 2 * side - 1},
            device_id_type=pl.DeviceIdType.MESH,
        )

    pairs = (
        (x_hbm, x_ref),
        (gain1_hbm, gain1_ref),
        (reach_hbm, reach_ref),
        (prof_hbm, prof_ref),
        (mix_hbm, mix_ref),
        (gain2_hbm, gain2_ref),
        (proj_hbm, proj_ref),
        (scale_hbm, scale_ref),
        (final_hbm, final_ref),
    )
    fetch = [
        pltpu.make_async_copy(source, target, loads.at[i])
        for i, (source, target) in enumerate(pairs)
    ]
    for copy in fetch:
        copy.start()

    barrier = pltpu.get_barrier_semaphore()
    for side in range(2):

        @pl.when(present(side))
        def _():
            pl.semaphore_signal(
                barrier,
                inc=1,
                device_id={"band": me - 1 if side == 0 else me + 1},
                device_id_type=pl.DeviceIdType.MESH,
            )

    pl.semaphore_wait(barrier, jnp.where(me == 0, 1, 2) - jnp.where(me == n - 1, 1, 0))

    for side in range(2):

        @pl.when(present(side))
        def _():
            x_copy(side).start()

    shape2 = (HEAD_COUNT * QUERY_BLOCK, channels)
    sub = lax.broadcasted_iota(jnp.int32, shape2, 0)
    lane = lax.broadcasted_iota(jnp.int32, shape2, 1)
    heads[...] = jnp.where(sub // QUERY_BLOCK == lane // HEAD_WIDTH, 1.0, 0.0).astype(BF16)
    ones_blocks = heads if QUERY_BLOCK == HEAD_WIDTH else None

    key = lax.broadcasted_iota(jnp.int32, (QUERY_BLOCK, KEYS), 1)
    query = lax.broadcasted_iota(jnp.int32, (QUERY_BLOCK, KEYS), 0)
    fetch[2].wait()
    for r in range(rows):
        limit = jnp.zeros((QUERY_BLOCK, KEYS), jnp.int32)
        start = jnp.zeros((QUERY_BLOCK, KEYS), jnp.int32)
        for a in range(ROWS_A):
            inside = key >= a * KEY_WINDOW
            limit = jnp.where(inside, reach_ref[r, a], limit)
            start = jnp.where(inside, a * KEY_WINDOW, start)
        distance = jnp.abs(key - start - DISC_REACH - query)
        bias[r] = jnp.where(distance <= limit, 0.0, -1e30).astype(F32)

    fetch[0].wait()
    fetch[1].wait()
    gain1 = gain1_ref[...]

    for r in range(rows):
        ext[r + 1] = ring_pad(rms(x_ref[r].astype(F32), gain1)).astype(BF16)

    tap_lane = lax.broadcasted_iota(jnp.int32, (16, KEYS), 1)

    def build_filters(r):
        taps[...] = jnp.zeros_like(taps)
        taps[0:BASIS_COUNT, 0 : 3 * TAPS] = prof_ref[:, r, :]
        flat = taps[...]
        placed = jnp.zeros_like(flat)
        for a in range(3):
            begin = a * CONV_WINDOW + CONV_REACH
            moved = pltpu.roll(flat, begin - a * TAPS, axis=1) if begin - a * TAPS else flat
            offset = tap_lane - begin
            reach = jnp.minimum(reach_ref[r, PATCH_LAT_EXTENT - 1 + a], CONV_REACH)
            inside = jnp.abs(offset - CONV_REACH) <= reach
            placed = jnp.where(inside, moved, placed)
        for k in range(BASIS_COUNT):
            spread = jnp.broadcast_to(placed[k : k + 1], (CONV_BLOCK, KEYS))
            spread = pltpu.roll(spread, 0, axis=1, stride=1, stride_axis=0)
            toeplitz[k * CONV_BLOCK : (k + 1) * CONV_BLOCK] = spread.astype(BF16)

    fetch[3].wait()

    def conv_row(r, first=False, edge=None):
        build_filters(r)

        def conv_block(b, carry):
            at = pl.multiple_of(b * CONV_BLOCK, CONV_BLOCK)
            window = jnp.concatenate(
                [
                    ext[r, pl.ds(at, CONV_WINDOW)],
                    ext[r + 1, pl.ds(at, CONV_WINDOW)],
                    ext[r + 2, pl.ds(at, KEYS - 2 * CONV_WINDOW)],
                ],
                axis=0,
            )
            sums = jnp.dot(toeplitz[...], window, preferred_element_type=F32).astype(BF16)
            for k in range(BASIS_COUNT):
                basis[pl.ds(at, CONV_BLOCK), k * channels : (k + 1) * channels] = sums[
                    k * CONV_BLOCK : (k + 1) * CONV_BLOCK
                ]
            return carry

        lax.fori_loop(0, longitudes // CONV_BLOCK, conv_block, 0, unroll=2)
        if first:
            fetch[4].wait()
            fetch[5].wait()
            fetch[6].wait()
        gain2 = gain2_ref[...]
        mixed = jnp.dot(basis[...], mix_ref[...], preferred_element_type=F32)
        total = x_ref[r].astype(F32) + mixed
        hidden[r] = total
        normed = rms(total, gain2)
        att[r + depth] = ring_pad(normed).astype(BF16)
        queries[r] = unit(
            jnp.dot(
                normed.astype(BF16), proj_ref[:, 0:channels], preferred_element_type=F32
            )
        )

        def share(side, step, pole_slot):
            @pl.when(present(side))
            def _():
                a_copy(side, step).start()

            @pl.when(jnp.logical_not(present(side)))
            def _():
                att[pole_slot] = ring_pad(half_turn(normed)).astype(BF16)

        if edge is not None:
            share(edge, edge * (depth - 1), (1 - edge) * (depth - 1) + edge * (rows + depth))
        else:
            if r < depth:
                share(0, r, depth - 1 - r)
            if r >= rows - depth:
                share(1, r - (rows - depth), 2 * rows + depth - 1 - r)

    def unit(product):
        value = product.astype(BF16).astype(F32)
        square = value * value
        high = square.astype(BF16)
        low = (square - high.astype(F32)).astype(BF16)
        total = jnp.dot(high, ones_blocks[...], preferred_element_type=F32)
        total = total + jnp.dot(low, ones_blocks[...], preferred_element_type=F32)
        return (value * lax.rsqrt(total + EPSILON)).astype(BF16)

    def key_value(row):
        source = att[row]
        keys[row] = unit(
            jnp.dot(source, proj_ref[:, channels : 2 * channels], preferred_element_type=F32)
        )
        values[row] = jnp.dot(
            source, proj_ref[:, 2 * channels :], preferred_element_type=F32
        ).astype(BF16)

    def edge_row(side):
        row = side * (rows - 1)
        slot = side * (rows + 1)

        @pl.when(present(side))
        def _():
            x_copy(1 - side).wait_recv()
            ext[slot] = ring_pad(rms(xhalo[side].astype(F32), gain1)).astype(BF16)

        @pl.when(jnp.logical_not(present(side)))
        def _():
            ext[slot] = ring_pad(half_turn(rms(x_ref[row].astype(F32), gain1))).astype(BF16)

        conv_row(row, edge=side)

    for r in range(1, rows - 1):
        conv_row(r, r == 1)
    edge_row(far)
    edge_row(near)

    for r in range(rows):
        key_value(r + depth)
    fetch[7].wait()
    fetch[8].wait()

    def halo_row(side, step):
        @pl.when(present(side))
        def _():
            a_copy(1 - side, step).wait_recv()

        row = side * (rows + depth) + step
        att[row, longitudes:] = att[row, 0 : PAD + TAIL]
        key_value(row)

    def halo_rows(side):
        for inner in range(depth):
            halo_row(side, side * (depth - 1 - 2 * inner) + inner)

    head_lane = lax.broadcasted_iota(jnp.int32, (QUERY_BLOCK, channels), 1) // HEAD_WIDTH
    sizes = [KEY_WINDOW] * (ROWS_A - 1) + [KEYS - (ROWS_A - 1) * KEY_WINDOW]

    def attend(r, starts):
        def windows(ref, at):
            return jnp.concatenate(
                [ref[r + a, pl.ds(at, sizes[a])] for a in range(ROWS_A)], axis=0
            )

        seen = bias[r]
        all_scores = []
        for at in starts:
            probe = queries[r, pl.ds(at, QUERY_BLOCK)]
            spread = jnp.concatenate([probe] * HEAD_COUNT, axis=0) * heads[...]
            all_scores.append(
                lax.dot_general(
                    spread,
                    windows(keys, at),
                    (((1,), (1,)), ((), ())),
                    preferred_element_type=F32,
                )
            )
        all_mixed, all_sums = [], []
        for at, scores in zip(starts, all_scores):
            parts, sums = [], []
            for h in range(HEAD_COUNT):
                part = scores[h * QUERY_BLOCK : (h + 1) * QUERY_BLOCK] + seen
                peak = jnp.max(part, axis=-1, keepdims=True)
                part = jnp.exp2((part - peak) * (scale_ref[h] * LOG2E))
                sums.append(jnp.sum(part, axis=-1, keepdims=True))
                parts.append(part.astype(BF16))
            all_mixed.append(
                jnp.dot(
                    jnp.concatenate(parts, axis=0),
                    windows(values, at),
                    preferred_element_type=F32,
                )
            )
            all_sums.append(sums)
        for at, mixed, sums in zip(starts, all_mixed, all_sums):
            result = jnp.zeros((QUERY_BLOCK, channels), F32)
            for h in range(HEAD_COUNT):
                share = mixed[h * QUERY_BLOCK : (h + 1) * QUERY_BLOCK] * (1.0 / sums[h])
                result = jnp.where(head_lane == h, share, result)
            mixture[pl.ds(at, QUERY_BLOCK)] = result.astype(BF16)

    group = GROUP
    while longitudes % (group * QUERY_BLOCK):
        group -= 1

    def attend_row(r):
        def attend_group(b, carry):
            at = pl.multiple_of(b * (group * QUERY_BLOCK), QUERY_BLOCK)
            attend(r, [at + g * QUERY_BLOCK for g in range(group)])
            return carry

        lax.fori_loop(0, longitudes // (group * QUERY_BLOCK), attend_group, 0)
        out_ref[r] = (
            hidden[r] + jnp.dot(mixture[...], final_ref[...], preferred_element_type=F32)
        ).astype(BF16)

    halo_rows(near)
    attend_row(near * (rows - 1))
    halo_rows(far)
    for r in range(1, rows - 1):
        attend_row(r)
    attend_row(far * (rows - 1))

    for side in range(2):

        @pl.when(present(side))
        def _():
            x_copy(side).wait_send()
            for step in range(depth):
                a_copy(side, step).wait_send()


def on_device(
    grid_inputs,
    stencil_prenorm_scale,
    patch_kernel_profiles,
    channel_mixer_tensor,
    softmax_prenorm_scale,
    probe_lookup_content_projector,
    head_logit_scales,
    final_projector,
    azimuth_reaches,
    *,
    n,
):
    rows, longitudes, channels = grid_inputs.shape
    padded = longitudes + PAD + TAIL
    wide = rows + 2 * PATCH_LAT_EXTENT
    vmem = pl.BlockSpec(memory_space=pltpu.VMEM)
    hbm = pl.BlockSpec(memory_space=pltpu.HBM)
    return pl.pallas_call(
        functools.partial(kernel, n),
        out_shape=pltpu.VMEM(grid_inputs.shape, BF16),
        in_specs=[hbm] * 9,
        out_specs=vmem,
        scratch_shapes=[
            pltpu.VMEM(grid_inputs.shape, BF16),
            pltpu.VMEM((1, channels), F32),
            pltpu.VMEM((patch_kernel_profiles.shape[1], rows, 3 * TAPS), F32),
            pltpu.VMEM(channel_mixer_tensor.shape, BF16),
            pltpu.VMEM((1, channels), F32),
            pltpu.VMEM(probe_lookup_content_projector.shape, BF16),
            pltpu.SMEM(head_logit_scales.shape, F32),
            pltpu.VMEM(final_projector.shape, BF16),
            pltpu.SMEM(azimuth_reaches.shape, jnp.int32),
            pltpu.VMEM((2, longitudes, channels), BF16),
            pltpu.VMEM((rows + 2, padded, channels), BF16),
            pltpu.VMEM((16, KEYS), F32),
            pltpu.VMEM((BASIS_COUNT * CONV_BLOCK, KEYS), BF16),
            pltpu.VMEM((longitudes, BASIS_COUNT * channels), BF16),
            pltpu.VMEM((rows, longitudes, channels), F32),
            pltpu.VMEM((wide, padded, channels), BF16),
            pltpu.VMEM((rows, longitudes, channels), BF16),
            pltpu.VMEM((wide, padded, channels), BF16),
            pltpu.VMEM((wide, padded, channels), BF16),
            pltpu.VMEM((rows, QUERY_BLOCK, KEYS), F32),
            pltpu.VMEM((HEAD_COUNT * QUERY_BLOCK, channels), BF16),
            pltpu.VMEM((longitudes, channels), BF16),
            pltpu.SemaphoreType.DMA((2,)),
            pltpu.SemaphoreType.DMA((2,)),
            pltpu.SemaphoreType.DMA((2 * PATCH_LAT_EXTENT,)),
            pltpu.SemaphoreType.DMA((2 * PATCH_LAT_EXTENT,)),
            pltpu.SemaphoreType.DMA((9,)),
        ],
        compiler_params=pltpu.CompilerParams(
            collective_id=0, has_side_effects=True, vmem_limit_bytes=62 * 1024 * 1024
        ),
    )(
        grid_inputs,
        stencil_prenorm_scale.reshape(1, channels),
        patch_kernel_profiles.transpose(1, 0, 2),
        channel_mixer_tensor,
        softmax_prenorm_scale.reshape(1, channels),
        probe_lookup_content_projector,
        head_logit_scales,
        final_projector,
        azimuth_reaches,
    )


def solution(mesh):
    placed = (
        P(("members", "band"), None, None),
        P(),
        P("band", None, None),
        P(),
        P(),
        P(),
        P(),
        P(),
        P("band", None),
    )
    return jax.shard_map(
        functools.partial(on_device, n=mesh.shape["band"]),
        mesh=mesh,
        in_specs=placed,
        out_specs=P(("members", "band"), None, None),
        check_vma=False,
    )
```

```python
import functools
import math

import jax
import jax.numpy as jnp
from jax import lax
from jax.experimental import pallas as pl
from jax.experimental.pallas import tpu as pltpu
from jax.sharding import PartitionSpec as P

HEAD_COUNT = 8
HEAD_WIDTH = 32
BASIS_COUNT = 9
CONV_REACH = 4
PATCH_LAT_EXTENT = 2
DISC_REACH = 8
EPSILON = 1e-06

TAPS = 2 * CONV_REACH + 1
CONV_BLOCK = 64
CONV_WINDOW = CONV_BLOCK + 16
QUERY_BLOCK = 32
KEY_WINDOW = QUERY_BLOCK + 2 * DISC_REACH
KEYS = 256
GROUP = 6
ROWS_A = 2 * PATCH_LAT_EXTENT + 1
PAD = DISC_REACH
TAIL = 24
LOG2E = math.log2(math.e)
F32 = jnp.float32
BF16 = jnp.bfloat16


def rms(values, gain):
    inverse = lax.rsqrt(jnp.mean(values * values, axis=-1, keepdims=True) + EPSILON)
    return values * inverse * gain


def ring_pad(row):
    return jnp.concatenate([row[-PAD:], row, row[:TAIL]], axis=0)


def half_turn(row):
    half = row.shape[0] // 2
    return jnp.concatenate([row[half:], row[:half]], axis=0)


def kernel(
    n,
    x_hbm,
    gain1_hbm,
    prof_hbm,
    mix_hbm,
    gain2_hbm,
    proj_hbm,
    scale_hbm,
    final_hbm,
    reach_hbm,
    out_ref,
    x_ref,
    gain1_ref,
    prof_ref,
    mix_ref,
    gain2_ref,
    proj_ref,
    scale_ref,
    final_ref,
    reach_ref,
    xhalo,
    ext,
    taps,
    toeplitz,
    basis,
    hidden,
    att,
    queries,
    keys,
    values,
    bias,
    heads,
    mixture,
    send_x,
    recv_x,
    send_a,
    recv_a,
    loads,
):
    rows, longitudes, channels = x_ref.shape
    assert rows > PATCH_LAT_EXTENT
    me = lax.axis_index("band")
    depth = PATCH_LAT_EXTENT
    sent = longitudes
    far = lax.rem(me, 2)
    near = 1 - far

    def present(side):
        other = me + 2 * side - 1
        return jnp.logical_and(other >= 0, other < n)

    def x_copy(side):
        return pltpu.make_async_remote_copy(
            src_ref=x_hbm.at[side * (rows - 1)],
            dst_ref=xhalo.at[1 - side],
            send_sem=send_x.at[side],
            recv_sem=recv_x.at[1 - side],
            device_id={"band": me + 2 * side - 1},
            device_id_type=pl.DeviceIdType.MESH,
        )

    def a_copy(side, step):
        source = (1 - side) * depth + side * rows + step
        target = (1 - side) * (rows + depth) + step
        return pltpu.make_async_remote_copy(
            src_ref=att.at[source, pl.ds(0, sent)],
            dst_ref=att.at[target, pl.ds(0, sent)],
            send_sem=send_a.at[side * depth + step],
            recv_sem=recv_a.at[(1 - side) * depth + step],
            device_id={"band": me + 2 * side - 1},
            device_id_type=pl.DeviceIdType.MESH,
        )

    pairs = (
        (x_hbm, x_ref),
        (gain1_hbm, gain1_ref),
        (reach_hbm, reach_ref),
        (prof_hbm, prof_ref),
        (mix_hbm, mix_ref),
        (gain2_hbm, gain2_ref),
        (proj_hbm, proj_ref),
        (scale_hbm, scale_ref),
        (final_hbm, final_ref),
    )
    fetch = [
        pltpu.make_async_copy(source, target, loads.at[i])
        for i, (source, target) in enumerate(pairs)
    ]
    for copy in fetch:
        copy.start()

    barrier = pltpu.get_barrier_semaphore()
    for side in range(2):

        @pl.when(present(side))
        def _():
            pl.semaphore_signal(
                barrier,
                inc=1,
                device_id={"band": me - 1 if side == 0 else me + 1},
                device_id_type=pl.DeviceIdType.MESH,
            )

    pl.semaphore_wait(barrier, jnp.where(me == 0, 1, 2) - jnp.where(me == n - 1, 1, 0))

    for side in range(2):

        @pl.when(present(side))
        def _():
            x_copy(side).start()

    shape2 = (HEAD_COUNT * QUERY_BLOCK, channels)
    sub = lax.broadcasted_iota(jnp.int32, shape2, 0)
    lane = lax.broadcasted_iota(jnp.int32, shape2, 1)
    heads[...] = jnp.where(sub // QUERY_BLOCK == lane // HEAD_WIDTH, 1.0, 0.0).astype(BF16)
    ones_blocks = heads if QUERY_BLOCK == HEAD_WIDTH else None

    key = lax.broadcasted_iota(jnp.int32, (QUERY_BLOCK, KEYS), 1)
    query = lax.broadcasted_iota(jnp.int32, (QUERY_BLOCK, KEYS), 0)
    fetch[2].wait()
    for r in range(rows):
        limit = jnp.zeros((QUERY_BLOCK, KEYS), jnp.int32)
        start = jnp.zeros((QUERY_BLOCK, KEYS), jnp.int32)
        for a in range(ROWS_A):
            inside = key >= a * KEY_WINDOW
            limit = jnp.where(inside, reach_ref[r, a], limit)
            start = jnp.where(inside, a * KEY_WINDOW, start)
        distance = jnp.abs(key - start - DISC_REACH - query)
        bias[r] = jnp.where(distance <= limit, 0.0, -1e30).astype(F32)

    fetch[0].wait()
    fetch[1].wait()
    gain1 = gain1_ref[...]

    for r in range(rows):
        ext[r + 1] = ring_pad(rms(x_ref[r].astype(F32), gain1)).astype(BF16)

    tap_lane = lax.broadcasted_iota(jnp.int32, (16, KEYS), 1)

    def build_filters(r):
        taps[...] = jnp.zeros_like(taps)
        taps[0:BASIS_COUNT, 0 : 3 * TAPS] = prof_ref[:, r, :]
        flat = taps[...]
        placed = jnp.zeros_like(flat)
        for a in range(3):
            begin = a * CONV_WINDOW + CONV_REACH
            moved = pltpu.roll(flat, begin - a * TAPS, axis=1) if begin - a * TAPS else flat
            offset = tap_lane - begin
            reach = jnp.minimum(reach_ref[r, PATCH_LAT_EXTENT - 1 + a], CONV_REACH)
            inside = jnp.abs(offset - CONV_REACH) <= reach
            placed = jnp.where(inside, moved, placed)
        for k in range(BASIS_COUNT):
            spread = jnp.broadcast_to(placed[k : k + 1], (CONV_BLOCK, KEYS))
            spread = pltpu.roll(spread, 0, axis=1, stride=1, stride_axis=0)
            toeplitz[k * CONV_BLOCK : (k + 1) * CONV_BLOCK] = spread.astype(BF16)

    fetch[3].wait()

    def conv_row(r, first=False, edge=None):
        if edge is None:
            build_filters(r)

        def conv_block(b, carry):
            at = pl.multiple_of(b * CONV_BLOCK, CONV_BLOCK)
            window = jnp.concatenate(
                [
                    ext[r, pl.ds(at, CONV_WINDOW)],
                    ext[r + 1, pl.ds(at, CONV_WINDOW)],
                    ext[r + 2, pl.ds(at, KEYS - 2 * CONV_WINDOW)],
                ],
                axis=0,
            )
            sums = jnp.dot(toeplitz[...], window, preferred_element_type=F32).astype(BF16)
            for k in range(BASIS_COUNT):
                basis[pl.ds(at, CONV_BLOCK), k * channels : (k + 1) * channels] = sums[
                    k * CONV_BLOCK : (k + 1) * CONV_BLOCK
                ]
            return carry

        lax.fori_loop(0, longitudes // CONV_BLOCK, conv_block, 0, unroll=2)
        if first:
            fetch[4].wait()
            fetch[5].wait()
            fetch[6].wait()
        gain2 = gain2_ref[...]
        mixed = jnp.dot(basis[...], mix_ref[...], preferred_element_type=F32)
        total = x_ref[r].astype(F32) + mixed
        hidden[r] = total
        normed = rms(total, gain2)
        att[r + depth] = ring_pad(normed).astype(BF16)
        queries[r] = unit(
            jnp.dot(
                normed.astype(BF16), proj_ref[:, 0:channels], preferred_element_type=F32
            )
        )

        def share(side, step, pole_slot):
            @pl.when(present(side))
            def _():
                a_copy(side, step).start()

            @pl.when(jnp.logical_not(present(side)))
            def _():
                att[pole_slot] = ring_pad(half_turn(normed)).astype(BF16)

        if edge is not None:
            share(edge, edge * (depth - 1), (1 - edge) * (depth - 1) + edge * (rows + depth))
        else:
            if r < depth:
                share(0, r, depth - 1 - r)
            if r >= rows - depth:
                share(1, r - (rows - depth), 2 * rows + depth - 1 - r)

    def unit(product):
        value = product.astype(BF16).astype(F32)
        square = value * value
        high = square.astype(BF16)
        low = (square - high.astype(F32)).astype(BF16)
        total = jnp.dot(high, ones_blocks[...], preferred_element_type=F32)
        total = total + jnp.dot(low, ones_blocks[...], preferred_element_type=F32)
        return (value * lax.rsqrt(total + EPSILON)).astype(BF16)

    def key_value(row):
        source = att[row]
        keys[row] = unit(
            jnp.dot(source, proj_ref[:, channels : 2 * channels], preferred_element_type=F32)
        )
        values[row] = jnp.dot(
            source, proj_ref[:, 2 * channels :], preferred_element_type=F32
        ).astype(BF16)

    def edge_row(side):
        row = side * (rows - 1)
        slot = side * (rows + 1)
        build_filters(row)

        @pl.when(present(side))
        def _():
            x_copy(1 - side).wait_recv()
            ext[slot] = ring_pad(rms(xhalo[side].astype(F32), gain1)).astype(BF16)

        @pl.when(jnp.logical_not(present(side)))
        def _():
            ext[slot] = ring_pad(half_turn(rms(x_ref[row].astype(F32), gain1))).astype(BF16)

        conv_row(row, edge=side)

    for r in range(1, rows - 1):
        conv_row(r, r == 1)
        key_value(r + depth)
    edge_row(far)
    edge_row(near)

    key_value(depth)
    key_value(rows - 1 + depth)
    fetch[7].wait()
    fetch[8].wait()

    def halo_row(side, step):
        @pl.when(present(side))
        def _():
            a_copy(1 - side, step).wait_recv()

        row = side * (rows + depth) + step
        att[row, longitudes:] = att[row, 0 : PAD + TAIL]
        key_value(row)

    def halo_rows(side):
        for inner in range(depth):
            halo_row(side, side * (depth - 1 - 2 * inner) + inner)

    head_lane = lax.broadcasted_iota(jnp.int32, (QUERY_BLOCK, channels), 1) // HEAD_WIDTH
    sizes = [KEY_WINDOW] * (ROWS_A - 1) + [KEYS - (ROWS_A - 1) * KEY_WINDOW]

    def attend(r, starts):
        def windows(ref, at):
            return jnp.concatenate(
                [ref[r + a, pl.ds(at, sizes[a])] for a in range(ROWS_A)], axis=0
            )

        seen = bias[r]
        all_scores = []
        for at in starts:
            probe = queries[r, pl.ds(at, QUERY_BLOCK)]
            spread = jnp.concatenate([probe] * HEAD_COUNT, axis=0) * heads[...]
            all_scores.append(
                lax.dot_general(
                    spread,
                    windows(keys, at),
                    (((1,), (1,)), ((), ())),
                    preferred_element_type=F32,
                )
            )
        all_mixed, all_sums = [], []
        for at, scores in zip(starts, all_scores):
            parts, sums = [], []
            for h in range(HEAD_COUNT):
                part = scores[h * QUERY_BLOCK : (h + 1) * QUERY_BLOCK] + seen
                peak = jnp.max(part, axis=-1, keepdims=True)
                part = jnp.exp2((part - peak) * (scale_ref[h] * LOG2E))
                sums.append(jnp.sum(part, axis=-1, keepdims=True))
                parts.append(part.astype(BF16))
            all_mixed.append(
                jnp.dot(
                    jnp.concatenate(parts, axis=0),
                    windows(values, at),
                    preferred_element_type=F32,
                )
            )
            all_sums.append(sums)
        for at, mixed, sums in zip(starts, all_mixed, all_sums):
            result = jnp.zeros((QUERY_BLOCK, channels), F32)
            for h in range(HEAD_COUNT):
                share = mixed[h * QUERY_BLOCK : (h + 1) * QUERY_BLOCK] * (1.0 / sums[h])
                result = jnp.where(head_lane == h, share, result)
            mixture[pl.ds(at, QUERY_BLOCK)] = result.astype(BF16)

    group = GROUP
    while longitudes % (group * QUERY_BLOCK):
        group -= 1

    def attend_row(r):
        def attend_group(b, carry):
            at = pl.multiple_of(b * (group * QUERY_BLOCK), QUERY_BLOCK)
            attend(r, [at + g * QUERY_BLOCK for g in range(group)])
            return carry

        lax.fori_loop(0, longitudes // (group * QUERY_BLOCK), attend_group, 0)
        out_ref[r] = (
            hidden[r] + jnp.dot(mixture[...], final_ref[...], preferred_element_type=F32)
        ).astype(BF16)

    halo_rows(near)
    attend_row(near * (rows - 1))
    halo_rows(far)
    for r in range(1, rows - 1):
        attend_row(r)
    attend_row(far * (rows - 1))

    for side in range(2):

        @pl.when(present(side))
        def _():
            x_copy(side).wait_send()
            for step in range(depth):
                a_copy(side, step).wait_send()


def on_device(
    grid_inputs,
    stencil_prenorm_scale,
    patch_kernel_profiles,
    channel_mixer_tensor,
    softmax_prenorm_scale,
    probe_lookup_content_projector,
    head_logit_scales,
    final_projector,
    azimuth_reaches,
    *,
    n,
):
    rows, longitudes, channels = grid_inputs.shape
    padded = longitudes + PAD + TAIL
    wide = rows + 2 * PATCH_LAT_EXTENT
    vmem = pl.BlockSpec(memory_space=pltpu.VMEM)
    hbm = pl.BlockSpec(memory_space=pltpu.HBM)
    return pl.pallas_call(
        functools.partial(kernel, n),
        out_shape=pltpu.VMEM(grid_inputs.shape, BF16),
        in_specs=[hbm] * 9,
        out_specs=vmem,
        scratch_shapes=[
            pltpu.VMEM(grid_inputs.shape, BF16),
            pltpu.VMEM((1, channels), F32),
            pltpu.VMEM((patch_kernel_profiles.shape[1], rows, 3 * TAPS), F32),
            pltpu.VMEM(channel_mixer_tensor.shape, BF16),
            pltpu.VMEM((1, channels), F32),
            pltpu.VMEM(probe_lookup_content_projector.shape, BF16),
            pltpu.SMEM(head_logit_scales.shape, F32),
            pltpu.VMEM(final_projector.shape, BF16),
            pltpu.SMEM(azimuth_reaches.shape, jnp.int32),
            pltpu.VMEM((2, longitudes, channels), BF16),
            pltpu.VMEM((rows + 2, padded, channels), BF16),
            pltpu.VMEM((16, KEYS), F32),
            pltpu.VMEM((BASIS_COUNT * CONV_BLOCK, KEYS), BF16),
            pltpu.VMEM((longitudes, BASIS_COUNT * channels), BF16),
            pltpu.VMEM((rows, longitudes, channels), F32),
            pltpu.VMEM((wide, padded, channels), BF16),
            pltpu.VMEM((rows, longitudes, channels), BF16),
            pltpu.VMEM((wide, padded, channels), BF16),
            pltpu.VMEM((wide, padded, channels), BF16),
            pltpu.VMEM((rows, QUERY_BLOCK, KEYS), F32),
            pltpu.VMEM((HEAD_COUNT * QUERY_BLOCK, channels), BF16),
            pltpu.VMEM((longitudes, channels), BF16),
            pltpu.SemaphoreType.DMA((2,)),
            pltpu.SemaphoreType.DMA((2,)),
            pltpu.SemaphoreType.DMA((2 * PATCH_LAT_EXTENT,)),
            pltpu.SemaphoreType.DMA((2 * PATCH_LAT_EXTENT,)),
            pltpu.SemaphoreType.DMA((9,)),
        ],
        compiler_params=pltpu.CompilerParams(
            collective_id=0, has_side_effects=True, vmem_limit_bytes=62 * 1024 * 1024
        ),
    )(
        grid_inputs,
        stencil_prenorm_scale.reshape(1, channels),
        patch_kernel_profiles.transpose(1, 0, 2),
        channel_mixer_tensor,
        softmax_prenorm_scale.reshape(1, channels),
        probe_lookup_content_projector,
        head_logit_scales,
        final_projector,
        azimuth_reaches,
    )


def solution(mesh):
    placed = (
        P(("members", "band"), None, None),
        P(),
        P("band", None, None),
        P(),
        P(),
        P(),
        P(),
        P(),
        P("band", None),
    )
    return jax.shard_map(
        functools.partial(on_device, n=mesh.shape["band"]),
        mesh=mesh,
        in_specs=placed,
        out_specs=P(("members", "band"), None, None),
        check_vma=False,
    )
```
